128 devices in a mesh: req: 16 (over z, x), head: 8 (over y, core).
Axes of the slice: x: 4, y: 4, z: 4, core: 2. Of those that a mesh axis runs over, the one named last changes fastest.
Arguments:
- embedded: bfloat16 [2, 96, 8192], P(None, None, 'req'), may hold values from -6 to 6
- ssm_states: bfloat16 [2, 192, 128, 128, 128], P(None, 'req', 'head'), may hold values from -0.59765625 to 0.59765625
- conv_tail_x: bfloat16 [2, 192, 3, 16384], P(None, 'req', None, 'head'), may hold values from -6 to 6
- conv_tail_bc: bfloat16 [2, 192, 3, 2048], P(None, 'req', None, 'head'), may hold values from -6 to 6
- prefill_slot: int32 [96], replicated, may hold values from 0 to 191, as said below
- decode_slot: int32 [96], replicated, may hold values from 0 to 95, as said below
- norm_gain: float32 [2, 8192], P(None, 'req'), may hold values from 0.5 to 1.5
- w_gate: bfloat16 [2, 8192, 16384], P(None, 'req', 'head'), may hold values from -0.0625 to 0.0625
- w_input: bfloat16 [2, 8192, 16384], P(None, 'req', 'head'), may hold values from -0.0625 to 0.0625
- w_groups: bfloat16 [2, 8192, 2048], P(None, 'req', 'head'), may hold values from -0.0625 to 0.0625
- w_step: bfloat16 [2, 8192, 128], P(None, 'req', 'head'), may hold values from -0.0625 to 0.0625
- conv_input: float32 [2, 4, 16384], P(None, None, 'head'), may hold values from -3 to 3
- conv_groups: float32 [2, 4, 2048], P(None, None, 'head'), may hold values from -3 to 3
- step_bias: float32 [2, 128], P(None, 'head'), may hold values from -3 to 0
- decay_rate: float32 [2, 128], P(None, 'head'), may hold values from 0.05 to 5
- skip_gain: float32 [2, 128], P(None, 'head'), may hold values from 0.5 to 1.5
- out_gain: float32 [2, 16384], P(None, 'head'), may hold values from 0.5 to 1.5
- w_output: bfloat16 [2, 16384, 8192], P(None, 'head', 'req'), may hold values from -0.046875 to 0.046875
Outputs:
- decoded: bfloat16 [2, 96, 8192], P(None, None, 'req')
The draws below stay inside these ranges and needn't reach their ends.
Inputs may be any that keep to these rules, and one draw needn't show every extreme that they name: `prefill_slot`: distinct slots; the slots of prefill owner q are q * 12 to q * 12 + 11, and some owner has all 12 slots used. No two requests with the same prefill owner have the same decode owner (decode_slot // 6). `decode_slot`: A permutation of the requests' rows.
All inputs are finite; a program needn't handle non-finite values.
Results may differ from the reference program's by a relative error of at most 0.008.
Values may be sent and summed in bfloat16 or wider, within the bound.
A program may use at most 256 MiB of HBM per device.

```python
import math
import jax
import jax.numpy as jnp
from jax import lax

D = 8192
H = 128
P_SIZE = 128
N = 128
G = 8
L = 2
STEPS = 2
REQ_DEV = 6
DI = 16384
HG = 16
CAP = 12
REQS = 96
SLOTS = 192
N_REQ = 16


def routing_tables(key):
    key_heavy, key_order, key_turn, key_perm = jax.random.split(key, 4)
    heavy = jax.random.randint(key_heavy, (), 0, N_REQ)
    order = jax.random.permutation(key_order, N_REQ)
    position = jnp.zeros((N_REQ,), jnp.int32).at[order].set(jnp.arange(N_REQ, dtype=jnp.int32))
    takes_heavy = (position < CAP).astype(jnp.int32)
    needed = REQ_DEV - takes_heavy
    starts = jnp.cumsum(needed) - needed
    row_ids = jnp.arange(REQS, dtype=jnp.int32)
    owner = row_ids // REQ_DEV
    within = row_ids % REQ_DEV
    other_pos = (starts[owner] + within - takes_heavy[owner]) % (N_REQ - 1)
    other_src = (heavy + 1 + other_pos) % N_REQ
    source = jnp.where((within == 0) & (takes_heavy[owner] == 1), heavy, other_src)
    earlier = (source[None, :] == source[:, None]) & (row_ids[None, :] < row_ids[:, None])
    rank = jnp.sum(earlier.astype(jnp.int32), axis=1)
    turn = jax.random.randint(key_turn, (N_REQ,), 0, CAP)
    row_slot = source * CAP + (rank + turn[source]) % CAP
    perm = jax.random.permutation(key_perm, REQS).astype(jnp.int32)
    return (row_slot[perm].astype(jnp.int32), perm)


def draw_prefill_slot(key, part):
    tables = routing_tables(key)
    return tables[0]


def draw_decode_slot(key, part):
    tables = routing_tables(key)
    return tables[1]


def strengthened(values, own_key, source, target, shards_of, factor):
    def block_of(dim):
        return (jnp.arange(values.shape[dim]) // (values.shape[dim] // shards_of)).reshape((-1,) + (1,) * (values.ndim - 1 - dim))

    near = jax.random.permutation(own_key, shards_of)[block_of(target)]
    second = (block_of(target) + shards_of // 2) % shards_of
    return jnp.where((block_of(source) == near) | (block_of(source) == second), factor * values, values)


def level_of(stream_key, shape, pieces, low, high):
    factor_of = 1.0
    for axis_at, blocks in pieces:
        draws = jax.random.uniform(jax.random.fold_in(jax.random.fold_in(stream_key, 6), axis_at), (blocks,), jnp.float32, low / len(pieces), high / len(pieces))
        factor_of = factor_of * jnp.repeat(jnp.exp(draws), shape[axis_at] // blocks).reshape((-1,) + (1,) * (len(shape) - 1 - axis_at))
    return factor_of


def bell_draw(rng, dims, deviation, limit, cuts=(), held_as=jnp.bfloat16):
    array = deviation * jax.random.normal(rng, dims, jnp.float32)
    if cuts:
        array = array * level_of(rng, dims, cuts, -0.22, 0.18)
    return jnp.clip(array, -limit, limit).astype(held_as)


def gaussian_with(key, shape, deviation, limit, cuts, heavy, kind=jnp.bfloat16):
    entries = deviation * jax.random.normal(key, shape, jnp.float32)
    if cuts:
        entries = entries * level_of(key, shape, cuts, -0.22, 0.18)
    return jnp.clip(strengthened(entries, jax.random.fold_in(key, 3), *heavy), -limit, limit).astype(kind)


def setup_inputs(seed: int = 0) -> dict:
    key_of = jax.random.split(jax.random.key(seed), 19)
    embedded = gaussian_with(key_of[0], (STEPS, REQS, D), 1.0, 6.0, ((2, 16),), (2, 1, 16, 2.0))
    ssm_states = bell_draw(key_of[1], (L, SLOTS, H, P_SIZE, N), 0.1, 0.59765625, ((1, 16), (2, 8)))
    conv_tail_x = bell_draw(key_of[2], (L, SLOTS, 3, DI), 1.0, 6.0, ((1, 16), (3, 8)))
    conv_tail_bc = bell_draw(key_of[3], (L, SLOTS, 3, 2 * G * N), 1.0, 6.0, ((1, 16), (3, 8)))
    prefill_slot = draw_prefill_slot(jax.random.fold_in(key_of[18], 71), 0)
    decode_slot = draw_decode_slot(jax.random.fold_in(key_of[18], 71), 0)
    norm_gain = jnp.clip(1.0 + 0.1 * jax.random.normal(key_of[6], (L, D), jnp.float32), 0.5, 1.5)
    w_gate = bell_draw(key_of[7], (L, D, DI), D ** -0.5, 0.0625, ((1, 16), (2, 8)))
    w_input = bell_draw(key_of[8], (L, D, DI), D ** -0.5, 0.0625, ((1, 16), (2, 8)))
    w_groups = bell_draw(key_of[9], (L, D, 2 * G * N), D ** -0.5, 0.0625, ((1, 16), (2, 8)))
    w_step = bell_draw(key_of[10], (L, D, H), D ** -0.5, 0.0625, ((1, 16), (2, 8)))
    conv_input = bell_draw(key_of[11], (L, 4, DI), 0.5, 3.0, ((2, 8),), jnp.float32)
    conv_groups = bell_draw(key_of[12], (L, 4, 2 * G * N), 0.5, 3.0, ((2, 8),), jnp.float32)
    step_bias = jnp.clip(-3.0 + 3.0 * jax.random.uniform(key_of[13], (L, H), jnp.float32) ** level_of(key_of[13], (L, H), ((1, 8),), -0.2, 0.2), -3.0, 0.0)
    decay_rate = jnp.clip(jnp.exp(math.log(5.0) - 4.6051702 * jax.random.uniform(key_of[14], (L, H), jnp.float32) ** level_of(key_of[14], (L, H), ((1, 8),), -0.2, 0.2)), 0.05, 5.0)
    skip_gain = jnp.clip(0.5 + 1.0 * jax.random.uniform(key_of[15], (L, H), jnp.float32) ** level_of(key_of[15], (L, H), ((1, 8),), -0.2, 0.2), 0.5, 1.5)
    out_gain = jnp.clip(1.0 + 0.1 * jax.random.normal(key_of[16], (L, DI), jnp.float32), 0.5, 1.5)
    w_output = bell_draw(key_of[17], (L, DI, D), DI ** -0.5, 0.046875, ((1, 8), (2, 16)))
    return dict(embedded=embedded, ssm_states=ssm_states, conv_tail_x=conv_tail_x, conv_tail_bc=conv_tail_bc, prefill_slot=prefill_slot, decode_slot=decode_slot, norm_gain=norm_gain, w_gate=w_gate, w_input=w_input, w_groups=w_groups, w_step=w_step, conv_input=conv_input, conv_groups=conv_groups, step_bias=step_bias, decay_rate=decay_rate, skip_gain=skip_gain, out_gain=out_gain, w_output=w_output)


epsilon = 1e-05

def ssm_rows(x_pre, bc_pre, dt_pre, states, tails_x, tails_bc, conv_in, conv_grp, bias, rate, skip):
    seq_x = jnp.concatenate([tails_x.astype(jnp.float32), x_pre[:, None, :]], axis=1)
    x_conv = jax.nn.silu(lax.optimization_barrier(jnp.sum(seq_x * conv_in[None], axis=1)))
    seq_bc = jnp.concatenate([tails_bc.astype(jnp.float32), bc_pre[:, None, :]], axis=1)
    bc_conv = jax.nn.silu(lax.optimization_barrier(jnp.sum(seq_bc * conv_grp[None], axis=1)))
    new_tx = jnp.concatenate([tails_x[:, 1:], x_pre.astype(jnp.bfloat16)[:, None, :]], axis=1)
    new_tbc = jnp.concatenate([tails_bc[:, 1:], bc_pre.astype(jnp.bfloat16)[:, None, :]], axis=1)
    rows = x_pre.shape[0]
    heads = dt_pre.shape[1]
    groups = bc_conv.shape[1] // (2 * N)
    pairs = bc_conv.reshape(rows, groups, 2 * N)
    b_head = jnp.repeat(pairs[:, :, :N], HG, axis=1)
    c_head = jnp.repeat(pairs[:, :, N:], HG, axis=1)
    delta = jax.nn.softplus(dt_pre + bias[None, :])
    decay = jnp.exp(-delta * rate[None, :])
    x_heads = x_conv.reshape(rows, heads, P_SIZE)
    new_states = decay[:, :, None, None] * states + (delta[:, :, None] * x_heads)[:, :, :, None] * b_head[:, :, None, :]
    result = jnp.einsum('rhpn,rhn->rhp', new_states, c_head, precision=lax.Precision.HIGHEST)
    result = result + skip[None, :, None] * x_heads
    return (result.reshape(rows, heads * P_SIZE), new_states, new_tx, new_tbc)

def gate_norm(ssm_out, gate_pre, gain):
    rows = ssm_out.shape[0]
    gated = ssm_out * jax.nn.silu(gate_pre)
    grouped = gated.reshape(rows, -1, DI // G)
    mean_sq = lax.optimization_barrier(jnp.mean(grouped * grouped, axis=2, keepdims=True))
    normed = (grouped * lax.rsqrt(mean_sq + epsilon)).reshape(rows, -1) * gain[None, :]
    return normed.astype(jnp.bfloat16)

def reference(embedded, ssm_states, conv_tail_x, conv_tail_bc, prefill_slot, decode_slot, norm_gain, w_gate, w_input, w_groups, w_step, conv_input, conv_groups, step_bias, decay_rate, skip_gain, out_gain, w_output):
    row_slot = jnp.zeros((REQS,), jnp.int32).at[decode_slot.astype(jnp.int32)].set(prefill_slot.astype(jnp.int32))
    streams = [embedded[step_idx].astype(jnp.float32) for step_idx in range(STEPS)]
    for layer_idx in range(L):
        cached = jnp.take(ssm_states[layer_idx], row_slot, axis=0).astype(jnp.float32)
        tails_x = jnp.take(conv_tail_x[layer_idx], row_slot, axis=0)
        tails_bc = jnp.take(conv_tail_bc[layer_idx], row_slot, axis=0)
        for step_idx in range(STEPS):
            stream = streams[step_idx]
            mean_sq = lax.optimization_barrier(jnp.mean(stream * stream, axis=1))
            normed = (stream * lax.rsqrt(mean_sq + epsilon)[:, None] * norm_gain[layer_idx][None, :]).astype(jnp.bfloat16)
            gate_pre = jnp.dot(normed, w_gate[layer_idx], preferred_element_type=jnp.float32)
            x_pre = jnp.dot(normed, w_input[layer_idx], preferred_element_type=jnp.float32)
            bc_pre = jnp.dot(normed, w_groups[layer_idx], preferred_element_type=jnp.float32)
            dt_pre = jnp.dot(normed, w_step[layer_idx], preferred_element_type=jnp.float32)
            ssm_out, cached, tails_x, tails_bc = ssm_rows(x_pre, bc_pre, dt_pre, cached, tails_x, tails_bc, conv_input[layer_idx], conv_groups[layer_idx], step_bias[layer_idx], decay_rate[layer_idx], skip_gain[layer_idx])
            normed_out = gate_norm(ssm_out, gate_pre, out_gain[layer_idx])
            streams[step_idx] = stream + jnp.dot(normed_out, w_output[layer_idx], preferred_element_type=jnp.float32)
    return jnp.stack([item.astype(jnp.bfloat16) for item in streams])
```

```python
import jax
import jax.numpy as jnp
from jax import lax
from jax.experimental import pallas as pl
from jax.experimental.pallas import tpu as pltpu
from jax.sharding import PartitionSpec as P

MESH = pl.DeviceIdType.MESH
F32 = jnp.float32
BF16 = jnp.bfloat16
EPS = 1e-05

L = 2
D = 8192
ROWS = 192
WIDTH = 512
CH = 2048
HALF = 2304
SUB = 1152
CAP = 12


def iota(shape, dim):
    return lax.broadcasted_iota(jnp.int32, shape, dim)


def div6(v):
    return (v * 43691) >> 18


def div12(v):
    return (v * 43691) >> 19


def div24(v):
    return (v * 43691) >> 20


def div48(v):
    return (v * 43691) >> 21


def hot(cond):
    return jnp.where(cond, 1.0, 0.0).astype(BF16)


def dot(a, b):
    return jnp.dot(a, b, preferred_element_type=F32)


def silu(v):
    return v / (1.0 + jnp.exp(-v))


def softplus(v):
    return jnp.maximum(v, 0.0) + jnp.log(1.0 + jnp.exp(-jnp.abs(v)))


def body(
    emb,
    states,
    tail_x,
    tail_bc,
    pslot,
    dslot,
    norm_gain,
    w_gate,
    w_input,
    w_groups,
    w_step,
    conv_in,
    conv_grp,
    bias,
    rate,
    skip,
    out_gain,
    w_output,
    out,
    wg,
    wi,
    wb,
    ws,
    wo,
    st,
    stream,
    perm_b,
    sel_a,
    sel_b,
    pick_a,
    pick_b,
    back,
    s1s,
    s1r,
    s2s,
    s2r,
    s3s,
    s3r,
    gat,
    acc,
    hs,
    hr,
    fin,
    load_sem,
    send_sem,
    recv_sem,
    hsend_sem,
    hrecv_sem,
):
    req = lax.axis_index("req")
    head = lax.axis_index("head")
    z = req // 4
    x = req % 4
    mine = (z, x)

    def peer(axis, k):
        if axis == 0:
            return ((z + k) % 4) * 4 + x
        return z * 4 + (x + k) % 4

    loads = []
    for l in range(L):
        row = [
            (w_gate.at[l], wg.at[l]),
            (w_step.at[l], ws.at[l]),
            (w_input.at[l], wi.at[l]),
            (w_groups.at[l], wb.at[l]),
            (states.at[l], st.at[l]),
            (w_output.at[l], wo.at[l]),
        ]
        loads.append([pltpu.make_async_copy(a, b, load_sem.at[l, i]) for i, (a, b) in enumerate(row)])
        for c in loads[l]:
            c.start()

    barrier = pltpu.get_barrier_semaphore()
    for k in (1, 2, 3):
        for axis in (0, 1):
            pl.semaphore_signal(barrier, inc=1, device_id=(peer(axis, k), head), device_id_type=MESH)
    for k in range(1, 8):
        pl.semaphore_signal(barrier, inc=1, device_id=(req, (head + k) % 8), device_id_type=MESH)

    e0 = emb[0].astype(F32)
    e1 = emb[1].astype(F32)
    for g in range(4):
        stream[48 * g : 48 * g + 24, :] = e0[24 * g : 24 * g + 24]
        stream[48 * g + 24 : 48 * g + 48, :] = e1[24 * g : 24 * g + 24]

    prow = pslot[...]
    drow = dslot[...]
    diag = iota((96, 96), 0) == iota((96, 96), 1)
    pcol = jnp.sum(jnp.where(diag, prow, 0), axis=1, keepdims=True)
    dcol = jnp.sum(jnp.where(diag, drow, 0), axis=1, keepdims=True)

    n = iota((1, ROWS), 1)
    g = div48(n)
    w = n - 48 * g
    s = div24(w)
    j = w - 24 * s
    jx = div6(j)
    perm_b[...] = hot(iota((ROWS, ROWS), 0) == 48 * jx + 24 * s + 6 * g + (j - 6 * jx))

    k = iota((1, 48), 1)
    ks = div24(k)
    kj = k - 24 * ks
    kg = div6(kj)
    p = iota((128, 1), 0)
    for half in (0, 1):
        r = 24 * z + kj if half == 0 else 24 * kg + 6 * x + (kj - 6 * kg)
        slot = jnp.sum(jnp.where(dcol == r, pcol, 0), axis=0, keepdims=True)
        q = div12(slot)
        first, second = p >> 5, (p >> 3) & 3
        pq = 4 * second + first if half == 0 else 4 * first + second
        key = (pq * 4 + ((p >> 1) & 3)) * 2 + (p & 1)
        (sel_a if half == 0 else sel_b)[...] = hot(key == (q * 4 + kg) * 2 + ks)

    def tables():
        t = iota((32, 1), 0)
        c = t & 15
        owner = jnp.sum(jnp.where(prow == CAP * req + c, div6(drow) + 1, 0), axis=1, keepdims=True) - 1
        owner = jnp.where(c < CAP, owner, -1)
        u = iota((1, 64), 1)
        src, ch, other, us = u >> 4, (u >> 3) & 1, (u >> 1) & 3, u & 1
        mine_key = jnp.where(owner >= 0, owner * 2 + (t >> 4), -1)
        for half in (0, 1):
            key = (4 * src + other if half == 0 else 4 * other + src) * 2 + us
            for cs in (0, 1):
                (pick_a if half == 0 else pick_b)[cs] = hot(mine_key == jnp.where(ch == cs, key, -2))
        m = iota((ROWS, 1), 0)
        mg = div48(m)
        mw = m - 48 * mg
        ms = div24(mw)
        r = 24 * mg + mw - 24 * ms
        slot = jnp.sum(jnp.where(drow == r, prow, 0), axis=1, keepdims=True)
        want = slot * 2 + ms
        v = iota((1, 768), 1)
        blk = div48(v)
        vw = v - 48 * blk
        vsub = div24(vw)
        vv = vw - 24 * vsub
        vs = div12(vv)
        vc = vv - 12 * vs
        for half in (0, 1):
            q = (blk & 3) * 4 + (blk >> 2) if half == 0 else blk
            key = (CAP * q + vc) * 2 + vs
            for sub in (0, 1):
                back[half, sub] = hot(want == jnp.where(vsub == sub, key, -1))

    wr = iota((48, 1), 0)
    wsub = div24(wr)
    wv = wr - 24 * wsub
    wst = div12(wv)
    compact = hot(iota((48, 64), 1) == 32 * wsub + 16 * wst + (wv - 12 * wst))

    place = hot(iota((16, 256), 0) == iota((16, 256), 1))

    pl.semaphore_wait(barrier, 13)

    pending = []

    def copy(src, dst, ss, rs, dev):
        return pltpu.make_async_remote_copy(
            src_ref=src, dst_ref=dst, send_sem=ss, recv_sem=rs, device_id=dev, device_id_type=MESH
        )

    def exchange(l, phase, half, send, recv):
        axis = (phase + half) % 2
        me = mine[axis]
        e = 2 * phase + half
        got = []
        for k in (2, 1, 3):
            c = copy(
                send.at[(me + k) % 4], recv.at[me],
                send_sem.at[l, e, k], recv_sem.at[l, e, k], (peer(axis, k), head),
            )
            c.start()
            pending.append(c)
            src = (me - k) % 4
            got.append((src, copy(
                send.at[src], recv.at[src],
                send_sem.at[l, e, k], recv_sem.at[l, e, k], (peer(axis, k), head),
            )))
        return got

    for l in range(L):
        gate_load, step_load, input_load, group_load, state_load, out_load = loads[l]
        x_now = stream[...]
        lhs_a = (x_now * norm_gain[l : l + 1, :]).astype(BF16)
        squares = jnp.sum(x_now * x_now, axis=1, keepdims=True)
        gate_load.wait()
        step_load.wait()

        def project(half, lhs, weight, count, base):
            def tile(i, _):
                cols = pl.ds(pl.multiple_of(i * 256, 256), 256)
                got = dot(lhs, weight[l, :, cols])
                for g in range(4):
                    s1s[l, half, g, :, cols] = got[48 * g : 48 * g + 48].astype(BF16)
                return 0
            lax.fori_loop(0, count, tile, 0)

        project(0, lhs_a, wg, 8, 0)
        small = dot(dot(lhs_a, ws[l]).astype(BF16), place)
        small = jnp.where(iota((ROWS, 256), 1) == 16, squares, small)
        for g in range(4):
            s1s[l, 0, g, :, CH:HALF] = small[48 * g : 48 * g + 48].astype(BF16)
        got_a = exchange(l, 0, 0, s1s.at[l, 0], s1r.at[l, 0])
        lhs_b = dot(perm_b[...], lhs_a).astype(BF16)
        input_load.wait()
        group_load.wait()
        project(1, lhs_b, wi, 8, 0)
        bc = dot(lhs_b, wb[l])
        for g in range(4):
            s1s[l, 1, g, :, CH:HALF] = bc[48 * g : 48 * g + 48].astype(BF16)
        got_b = exchange(l, 0, 1, s1s.at[l, 1], s1r.at[l, 1])
        if l == 0:
            tables()

        got2 = []
        for half, got in ((0, got_a), (1, got_b)):
            for _, c in got:
                c.wait_recv()
            sel = (sel_a if half == 0 else sel_b)[...]
            me = mine[half]
            for i in range(3):
                cols = slice(768 * i, 768 * i + 768)
                total = s1s[l, half, me, :, cols].astype(F32)
                for src, _ in got:
                    total += s1r[l, half, src, :, cols].astype(F32)
                put = dot(sel, total.astype(BF16)).astype(BF16)
                for g in range(4):
                    s2s[l, half, g, :, cols] = put[32 * g : 32 * g + 32]
            got2.append(exchange(l, 1, half, s2s.at[l, half], s2r.at[l, half]))

        got3 = []
        for half in (0, 1):
            for _, c in got2[half]:
                c.wait_recv()
            me = mine[1 - half]
            for i in range(3):
                lo = slice(384 * i, 384 * i + 384)
                hi = slice(SUB + 384 * i, SUB + 384 * i + 384)
                parts = []
                for cols in (lo, hi):
                    total = s2s[l, half, me, :, cols].astype(F32)
                    for src, _ in got2[half]:
                        total += s2r[l, half, src, :, cols].astype(F32)
                    parts.append(total)
                for g in range(4):
                    rows = slice(8 * g, 8 * g + 8)
                    both = jnp.concatenate([parts[0][rows], parts[1][rows]], axis=0)
                    s3s[l, half, g, :, lo] = both.astype(BF16)
            got3.append(exchange(l, 2, half, s3s.at[l, half], s3r.at[l, half]))

        landed = []
        for half in (0, 1):
            me = mine[half]
            for _, c in got3[half]:
                c.wait_recv()
            s3r[l, half, me] = s3s[l, half, me]
            block = s3r[l, half].reshape(64, SUB)
            pick = pick_a if half == 0 else pick_b
            landed.append([dot(pick[cs], block) for cs in (0, 1)])
        (ga, gb), (xa, xb) = landed
        small = gb[:, SUB - 256 :]
        scale = lax.rsqrt(small[:, 16:17] * (1.0 / D) + EPS)
        gate_pre = jnp.concatenate([ga, gb[:, : SUB - 256]], axis=1) * scale
        x_pre = jnp.concatenate([xa, xb[:, : SUB - 256]], axis=1) * scale
        bc_pre = xb[:, SUB - 256 :] * scale
        dt_pre = small[:, :16] * scale

        def conv(pre, tails, taps):
            t0, t1, t2 = (tails[l, i].astype(F32) for i in range(3))
            c0, c1, c2, c3 = (taps[l, i : i + 1, :] for i in range(4))
            p0, p1 = pre[:16], pre[16:]
            first = t0 * c0 + t1 * c1 + t2 * c2 + p0 * c3
            second = t1 * c0 + t2 * c1 + p0.astype(BF16).astype(F32) * c2 + p1 * c3
            return silu(first), silu(second)

        bc0, bc1 = conv(bc_pre, tail_bc, conv_grp)
        b0, c0 = bc0[:, :128], bc0[:, 128:]
        b1, c1 = bc1[:, :128], bc1[:, 128:]
        both_c = jnp.concatenate([c0, c1], axis=0).astype(BF16)
        slot_of = iota((32, 1), 0) & 15
        state_load.wait()
        acc[0:32, :] = jnp.zeros((32, CH), F32)

        def contract(c, _):
            lhs = jnp.where(slot_of == c, both_c, jnp.zeros((), BF16))
            acc[0:32, :] += lax.dot_general(
                lhs, st[l, c], (((1,), (1,)), ((), ())), preferred_element_type=F32
            )
            return 0

        lax.fori_loop(0, CAP, contract, 0)

        x0, x1 = conv(x_pre, tail_x, conv_in)
        delta = softplus(dt_pre + bias[l : l + 1, :])
        decay = jnp.exp(-delta * rate[l : l + 1, :])
        direct = skip[l : l + 1, :]
        dl0, dl1 = delta[:16], delta[16:]
        de0, de1 = decay[:16], decay[16:]
        k00 = dl0 * jnp.sum(b0 * c0, axis=1, keepdims=True) + direct
        k10 = de1 * dl0 * jnp.sum(b0 * c1, axis=1, keepdims=True)
        k11 = dl1 * jnp.sum(b1 * c1, axis=1, keepdims=True) + direct
        m1 = de1 * de0
        outs = []
        for h in range(16):
            cols = slice(128 * h, 128 * h + 128)
            one = slice(h, h + 1)
            y0 = de0[:, one] * acc[0:16, cols] + k00[:, one] * x0[:, cols]
            y1 = m1[:, one] * acc[16:32, cols] + k10[:, one] * x0[:, cols] + k11[:, one] * x1[:, cols]
            outs.append(jnp.concatenate([y0, y1], axis=0))
        gated = jnp.concatenate(outs, axis=1) * silu(gate_pre)
        mean_sq = jnp.sum(gated * gated, axis=1, keepdims=True) * (1.0 / CH)
        normed = (gated * lax.rsqrt(mean_sq + EPS) * out_gain[l : l + 1, :]).astype(BF16)

        for half in (0, 1):
            a, b = mine[1 - half], mine[half]
            cols = 1024 * half
            stacked = jnp.concatenate([normed[:, cols : cols + 512], normed[:, cols + 512 : cols + 1024]], axis=0)
            gat[l, half, a, b] = dot(compact, stacked).astype(BF16)
        gots = []
        for half in (0, 1):
            axis = half
            a, b = mine[1 - half], mine[half]
            e = 6 + half
            got = []
            for k in (2, 1, 3):
                sems = (send_sem.at[l, e, k], recv_sem.at[l, e, k], (peer(axis, k), head))
                c = copy(gat.at[l, half, a, b], gat.at[l, half, a, b], *sems)
                c.start()
                pending.append(c)
                src = (b - k) % 4
                got.append(copy(gat.at[l, half, a, src], gat.at[l, half, a, src], *sems))
            gots.append(got)
        lasts = []
        for half in (0, 1):
            axis = 1 - half
            a = mine[1 - half]
            e = 8 + half
            for c in gots[half]:
                c.wait_recv()
            got = []
            for k in (2, 1, 3):
                sems = (send_sem.at[l, e, k], recv_sem.at[l, e, k], (peer(axis, k), head))
                c = copy(gat.at[l, half, a], gat.at[l, half, a], *sems)
                c.start()
                pending.append(c)
                src = (a - k) % 4
                got.append(copy(gat.at[l, half, src], gat.at[l, half, src], *sems))
            lasts.append(got)
        out_load.wait()
        acc_now = acc.at[0:ROWS, 0:WIDTH]
        for half in (0, 1):
            for c in lasts[half]:
                c.wait_recv()
            rows = gat[l, half].reshape(768, 512)
            for sub in (0, 1):
                lhs = dot(back[half, sub], rows).astype(BF16)
                base = 1024 * half + 512 * sub
                part = dot(lhs, wo[l, base : base + 512, :])
                if half + sub == 0:
                    acc_now[...] = part
                else:
                    acc_now[...] += part

        for h in range(8):
            i, c = h // 4, h % 4
            hs[l, h] = acc[96 * i : 96 * i + 96, 128 * c : 128 * c + 128].astype(BF16)
        got = []
        for k in (4, 3, 5, 2, 6, 1, 7):
            dev = (req, (head + k) % 8)
            sems = (hsend_sem.at[l, 0, k], hrecv_sem.at[l, 0, k], dev)
            c = copy(hs.at[l, (head + k) % 8], hr.at[l, head], *sems)
            c.start()
            pending.append(c)
            src = (head - k) % 8
            got.append((src, copy(hs.at[l, src], hr.at[l, src], *sems)))
        total = hs[l, head].astype(F32)
        for src, c in got:
            c.wait_recv()
            total += hr[l, src].astype(F32)
        fin[l, head] = total.astype(BF16)
        got = []
        for k in (4, 3, 5, 2, 6, 1, 7):
            dev = (req, (head + k) % 8)
            sems = (hsend_sem.at[l, 1, k], hrecv_sem.at[l, 1, k], dev)
            c = copy(fin.at[l, head], fin.at[l, head], *sems)
            c.start()
            pending.append(c)
            src = (head - k) % 8
            got.append(copy(fin.at[l, src], fin.at[l, src], *sems))
        for c in got:
            c.wait_recv()
        for h in range(8):
            i, c = h // 4, h % 4
            stream[96 * i : 96 * i + 96, 128 * c : 128 * c + 128] += fin[l, h].astype(F32)

    whole = stream[...]
    for s in (0, 1):
        parts = [whole[48 * g + 24 * s : 48 * g + 24 * s + 24] for g in range(4)]
        out[s] = jnp.concatenate(parts, axis=0).astype(BF16)
    for c in pending:
        c.wait_send()


def on_device(
    embedded,
    ssm_states,
    conv_tail_x,
    conv_tail_bc,
    prefill_slot,
    decode_slot,
    norm_gain,
    w_gate,
    w_input,
    w_groups,
    w_step,
    conv_input,
    conv_groups,
    step_bias,
    decay_rate,
    skip_gain,
    out_gain,
    w_output,
):
    vmem = pl.BlockSpec(memory_space=pltpu.VMEM)
    hbm = pl.BlockSpec(memory_space=pl.ANY)

    def by_tap(tails):
        return jnp.pad(jnp.swapaxes(tails, 1, 2), ((0, 0), (0, 0), (0, 4), (0, 0)))

    return pl.pallas_call(
        body,
        out_shape=jax.ShapeDtypeStruct((2, 96, WIDTH), BF16),
        in_specs=[vmem, hbm, vmem, vmem, vmem, vmem, vmem, hbm, hbm, hbm, hbm, vmem, vmem, vmem, vmem, vmem, vmem, hbm],
        out_specs=vmem,
        scratch_shapes=[
            pltpu.VMEM((L, WIDTH, CH), BF16),
            pltpu.VMEM((L, WIDTH, CH), BF16),
            pltpu.VMEM((L, WIDTH, 256), BF16),
            pltpu.VMEM((L, WIDTH, 16), BF16),
            pltpu.VMEM((L, CH, WIDTH), BF16),
            pltpu.VMEM((L, CAP, CH, 128), BF16),
            pltpu.VMEM((ROWS, WIDTH), F32),
            pltpu.VMEM((ROWS, ROWS), BF16),
            pltpu.VMEM((128, 48), BF16),
            pltpu.VMEM((128, 48), BF16),
            pltpu.VMEM((2, 32, 64), BF16),
            pltpu.VMEM((2, 32, 64), BF16),
            pltpu.VMEM((2, 2, ROWS, 768), BF16),
            pltpu.VMEM((L, 2, 4, 48, HALF), BF16),
            pltpu.VMEM((L, 2, 4, 48, HALF), BF16),
            pltpu.VMEM((L, 2, 4, 32, HALF), BF16),
            pltpu.VMEM((L, 2, 4, 32, HALF), BF16),
            pltpu.VMEM((L, 2, 4, 16, SUB), BF16),
            pltpu.VMEM((L, 2, 4, 16, SUB), BF16),
            pltpu.VMEM((L, 2, 4, 4, 48, 512), BF16),
            pltpu.VMEM((ROWS, CH), F32),
            pltpu.VMEM((L, 8, 96, 128), BF16),
            pltpu.VMEM((L, 8, 96, 128), BF16),
            pltpu.VMEM((L, 8, 96, 128), BF16),
            pltpu.SemaphoreType.DMA((L, 6)),
            pltpu.SemaphoreType.DMA((L, 10, 4)),
            pltpu.SemaphoreType.DMA((L, 10, 4)),
            pltpu.SemaphoreType.DMA((L, 2, 8)),
            pltpu.SemaphoreType.DMA((L, 2, 8)),
        ],
        compiler_params=pltpu.CompilerParams(
            collective_id=0, has_side_effects=True, vmem_limit_bytes=58 * 2**20
        ),
    )(
        embedded,
        ssm_states.reshape(L, CAP, CH, 128),
        by_tap(conv_tail_x),
        by_tap(conv_tail_bc),
        prefill_slot.reshape(1, 96),
        decode_slot.reshape(1, 96),
        norm_gain,
        w_gate,
        w_input,
        w_groups,
        w_step,
        conv_input,
        conv_groups,
        step_bias,
        decay_rate,
        skip_gain,
        out_gain,
        w_output,
    )


def solution(mesh):
    return jax.shard_map(
        on_device,
        mesh=mesh,
        in_specs=(
            P(None, None, "req"),
            P(None, "req", "head", None, None),
            P(None, "req", None, "head"),
            P(None, "req", None, "head"),
            P(),
            P(),
            P(None, "req"),
            P(None, "req", "head"),
            P(None, "req", "head"),
            P(None, "req", "head"),
            P(None, "req", "head"),
            P(None, None, "head"),
            P(None, None, "head"),
            P(None, "head"),
            P(None, "head"),
            P(None, "head"),
            P(None, "head"),
            P(None, "head", "req"),
        ),
        out_specs=P(None, None, "req"),
        check_vma=False,
    )
```

```python
import jax
import jax.numpy as jnp
from jax import lax
from jax.experimental import pallas as pl
from jax.experimental.pallas import tpu as pltpu
from jax.sharding import PartitionSpec as P

MESH = pl.DeviceIdType.MESH
F32 = jnp.float32
BF16 = jnp.bfloat16
EPS = 1e-05

L = 2
D = 8192
ROWS = 96
WIDTH = 512
CH = 2048
S = 2
PART = 1152
CAP = 12


def iota(shape, dim):
    return lax.broadcasted_iota(jnp.int32, shape, dim)


def div6(v):
    return (v * 43691) >> 18


def div12(v):
    return (v * 43691) >> 19


def div24(v):
    return (v * 43691) >> 20


def div48(v):
    return (v * 43691) >> 21


def hot(cond):
    return jnp.where(cond, 1.0, 0.0).astype(BF16)


def dot(a, b):
    return jnp.dot(a, b, preferred_element_type=F32)


def dot_t(a, b):
    return lax.dot_general(a, b, (((1,), (1,)), ((), ())), preferred_element_type=F32)


def silu(v):
    return v / (1.0 + jnp.exp(-v))


def softplus(v):
    return jnp.maximum(v, 0.0) + jnp.log(1.0 + jnp.exp(-jnp.abs(v)))


def body(
    emb_h,
    states,
    tail_x_h,
    tail_bc_h,
    pslot_h,
    dslot_h,
    norm_gain_h,
    w_gate,
    w_input,
    w_groups,
    w_step,
    conv_in_h,
    conv_grp_h,
    bias_h,
    rate_h,
    skip_h,
    out_gain_h,
    w_output,
    out,
    emb,
    tail_x2,
    tail_bc2,
    pslot,
    dslot,
    norm_gain,
    conv_in,
    conv_grp,
    bias,
    rate,
    skip,
    out_gain,
    tail_x,
    tail_bc,
    small_sem,
    wg,
    wi,
    wb,
    ws,
    wo,
    st,
    stream,
    perm_b,
    sel_a,
    sel_b,
    pick_a,
    pick_b,
    back,
    s1s,
    s1r,
    s2s,
    s2r,
    s3s,
    s3r,
    gat,
    held,
    hs,
    hr,
    fin,
    load_sem,
    send_sem,
    recv_sem,
    gsend_sem,
    grecv_sem,
    hsend_sem,
    hrecv_sem,
):
    req = lax.axis_index("req")
    head = lax.axis_index("head")
    z = req // 4
    x = req % 4
    mine = (z, x)

    def peer(axis, k):
        if axis == 0:
            return ((z + k) % 4) * 4 + x
        return z * 4 + (x + k) % 4

    loads = []
    for l in range(L):
        row = [
            (w_gate.at[l], wg.at[l]),
            (w_step.at[l], ws.at[l]),
            (w_input.at[l], wi.at[l]),
            (w_groups.at[l], wb.at[l]),
            (states.at[l], st.at[l]),
            (w_output.at[l], wo.at[l]),
        ]
        loads.append([pltpu.make_async_copy(a, b, load_sem.at[l, i]) for i, (a, b) in enumerate(row)])
    first = [(pslot_h, pslot), (dslot_h, dslot), (emb_h, emb), (norm_gain_h, norm_gain)]
    later = [
        (tail_x_h, tail_x2),
        (tail_bc_h, tail_bc2),
        (conv_in_h, conv_in),
        (conv_grp_h, conv_grp),
        (bias_h, bias),
        (rate_h, rate),
        (skip_h, skip),
        (out_gain_h, out_gain),
    ]
    first = [pltpu.make_async_copy(a, b, small_sem.at[i]) for i, (a, b) in enumerate(first)]
    later = [pltpu.make_async_copy(a, b, small_sem.at[4 + i]) for i, (a, b) in enumerate(later)]
    for c in first + loads[0] + later:
        c.start()

    barrier = pltpu.get_barrier_semaphore()
    for k in (1, 2, 3):
        for axis in (0, 1):
            pl.semaphore_signal(barrier, inc=1, device_id=(peer(axis, k), head), device_id_type=MESH)
    for k in range(1, 8):
        pl.semaphore_signal(barrier, inc=1, device_id=(req, (head + k) % 8), device_id_type=MESH)

    for c in first:
        c.wait()

    for t in range(S):
        stream[t] = emb[t].astype(F32)

    prow = pslot[...]
    drow = dslot[...]
    diag = iota((96, 96), 0) == iota((96, 96), 1)
    pcol = jnp.sum(jnp.where(diag, prow, 0), axis=1, keepdims=True)
    dcol = jnp.sum(jnp.where(diag, drow, 0), axis=1, keepdims=True)

    n = iota((1, ROWS), 1)
    g = div24(n)
    j = n - 24 * g
    jx = div6(j)
    perm_b[...] = hot(iota((ROWS, ROWS), 0) == 24 * jx + 6 * g + (j - 6 * jx))

    k = iota((1, 48), 1)
    kp = div24(k)
    kj = k - 24 * kp
    kg = div6(kj)
    p = iota((128, 1), 0)
    for half in (0, 1):
        r = 24 * z + kj if half == 0 else 24 * kg + 6 * x + (kj - 6 * kg)
        slot = jnp.sum(jnp.where(dcol == r, pcol, 0), axis=0, keepdims=True)
        q = div12(slot)
        first, second = p >> 5, (p >> 3) & 3
        pq = 4 * second + first if half == 0 else 4 * first + second
        key = (pq * 4 + (p & 3)) * 2 + ((p >> 2) & 1)
        (sel_a if half == 0 else sel_b)[...] = hot(key == (q * 4 + kg) * 2 + kp)

    def tables():
        t = iota((32, 1), 0)
        c = t & 15
        owner = jnp.sum(jnp.where(prow == CAP * req + c, div6(drow) + 1, 0), axis=1, keepdims=True) - 1
        mine_key = jnp.where((owner >= 0) & (c < CAP), owner * 2 + (t >> 4), -1)
        u = iota((1, 32), 1)
        src, up, other = u >> 3, (u >> 2) & 1, u & 3
        for half in (0, 1):
            key = (4 * src + other if half == 0 else 4 * other + src) * 2 + up
            (pick_a if half == 0 else pick_b)[...] = hot(mine_key == key)
        want = jnp.sum(jnp.where(drow == iota((ROWS, 1), 0), prow, 0), axis=1, keepdims=True)
        v = iota((1, 768), 1)
        blk = div48(v)
        vw = v - 48 * blk
        vsub = div12(vw)
        vc = vw - 12 * vsub
        for half in (0, 1):
            q = (blk & 3) * 4 + (blk >> 2) if half == 0 else blk
            for sub in range(4):
                back[half, sub] = hot(want == jnp.where(vsub == sub, CAP * q + vc, -1))

    wr = iota((48, 1), 0)
    wsub = div12(wr)
    compact = hot(iota((48, 64), 1) == 16 * wsub + (wr - 12 * wsub))

    place = hot(iota((16, 128), 0) == iota((16, 128), 1))

    pl.semaphore_wait(barrier, 13)

    def drain(l, t, phase):
        for half in (0, 1):
            f = flights.pop((l, t, phase, half), None)
            if f is not None:
                f.wait_send()

    def copy(src, dst, ss, rs, dev):
        return pltpu.make_async_remote_copy(
            src_ref=src, dst_ref=dst, send_sem=ss, recv_sem=rs, device_id=dev, device_id_type=MESH
        )

    flights = {}
    others = {}

    def exchange(l, t, phase, half):
        send, recv = ((s1s, s1r), (s2s, s2r), (s3s, s3r))[phase]
        axis = (phase + half) % 2
        me = mine[axis]
        e = 2 * phase + half
        sems = (send_sem.at[t, e], recv_sem.at[t, e])
        for k in (2, 1, 3):
            copy(send.at[l, t, half, (me + k) % 4], recv.at[l, t, half, me], *sems, (peer(axis, k), head)).start()
        three = (send.at[l, t, half, 0:3], recv.at[l, t, half, 0:3])
        flights[l, t, phase, half] = copy(*three, *sems, (peer(axis, 1), head))
        others[l, t, phase, half] = [(me + k) % 4 for k in (1, 2, 3)]

    waited = set()

    def ready(l, i):
        if (l, i) not in waited:
            waited.add((l, i))
            loads[l][i].wait()

    def project(l, steps):
        many = len(steps)
        x_now = jnp.concatenate([stream[t] for t in steps], axis=0)
        lhs_a = (x_now * norm_gain[l : l + 1, :]).astype(BF16)
        lhs_b = jnp.concatenate(
            [dot(perm_b[...], lhs_a[ROWS * i : ROWS * i + ROWS]).astype(BF16) for i in range(many)], axis=0
        )
        squares = jnp.sum(x_now * x_now, axis=1, keepdims=True)

        def put(half, cols, low, high):
            for i, t in enumerate(steps):
                for g in range(4):
                    rows = slice(ROWS * i + 24 * g, ROWS * i + 24 * g + 24)
                    s1s[l, t, half, g, :, cols] = jnp.concatenate([low[rows], high[rows]], axis=0).astype(BF16)

        def main(half, lhs, weight):
            def tile(i, _):
                at = pl.multiple_of(i * 256, 256)
                low = dot(lhs, weight[l, :, pl.ds(at, 256)])
                high = dot(lhs, weight[l, :, pl.ds(pl.multiple_of(at + 1024, 256), 256)])
                put(half, pl.ds(at, 256), low, high)
                return 0

            lax.fori_loop(0, 4, tile, 0)

        end = slice(1024, PART)
        ready(l, 1)
        small = dot(dot_t(lhs_a, ws[l]).astype(BF16), place)
        small = jnp.where(iota((ROWS * many, 128), 1) == 16, squares, small)
        put(0, end, small, jnp.zeros_like(small))
        ready(l, 0)
        main(0, lhs_a, wg)
        for t in steps:
            exchange(l, t, 0, 0)
        ready(l, 3)
        bc = dot(lhs_b, wb[l])
        put(1, end, bc[:, :128], bc[:, 128:])
        ready(l, 2)
        main(1, lhs_b, wi)
        for t in steps:
            exchange(l, t, 0, 1)

    def second(l, t):
        for half in (0, 1):
            flights[l, t, 0, half].wait_recv()
            total = s1s[l, t, half, mine[half]].astype(F32)
            for src in others[l, t, 0, half]:
                total += s1r[l, t, half, src].astype(F32)
            put = dot((sel_a if half == 0 else sel_b)[...], total.astype(BF16)).astype(BF16)
            for g in range(4):
                s2s[l, t, half, g] = put[32 * g : 32 * g + 32]
            exchange(l, t, 1, half)

    def third(l, t):
        for half in (0, 1):
            flights[l, t, 1, half].wait_recv()
            total = s2s[l, t, half, mine[1 - half]].astype(F32)
            for src in others[l, t, 1, half]:
                total += s2r[l, t, half, src].astype(F32)
            for g in range(4):
                s3s[l, t, half, g] = total[8 * g : 8 * g + 8]
            exchange(l, t, 2, half)

    def landed(l, t, half):
        me = mine[half]
        flights[l, t, 2, half].wait_recv()
        s3r[l, t, half, me] = s3s[l, t, half, me]
        block = s3r[l, t, half].reshape(32, PART)
        pick = (pick_a if half == 0 else pick_b)[...]
        high = block.astype(BF16)
        low = (block - high.astype(F32)).astype(BF16)
        both = dot(pick, high) + dot(pick, low)
        main = jnp.concatenate([both[:16, :1024], both[16:, :1024]], axis=1)
        return main, both[:16, 1024:], both[16:, 1024:]

    kept = {}

    def conv(l, pre, old, tails, taps):
        tap = [taps[l, i : i + 1, :] for i in range(4)]
        tail = [tails[48 * l + 16 * i : 48 * l + 16 * i + 16, :] for i in range(3)]
        seq = (tail + [pre]) if old is None else (tail[1:] + [old.astype(BF16).astype(F32), pre])
        return silu(seq[0] * tap[0] + seq[1] * tap[1] + seq[2] * tap[2] + seq[3] * tap[3])

    def scan(l, t):
        xm, xb, xc = landed(l, t, 1)
        gm, small, _ = landed(l, t, 0)
        scale = lax.rsqrt(small[:, 16:17] * (1.0 / D) + EPS)
        dt_pre = small[:, :16] * scale
        bc_pre = jnp.concatenate([xb, xc], axis=1) * scale
        x_pre = xm * scale
        old = kept.get(l)
        bc = conv(l, bc_pre, old and old[0], tail_bc, conv_grp)
        b_now, c_now = bc[:, :128], bc[:, 128:]
        c_low = c_now.astype(BF16)
        slot_of = iota((16, 1), 0)
        ready(l, 4)
        held[...] = jnp.zeros_like(held)

        zero = jnp.zeros((), BF16)

        def contract(i, _):
            c = 2 * i
            lhs = jnp.concatenate([jnp.where(slot_of == c, c_low, zero), jnp.where(slot_of == c + 1, c_low, zero)], axis=1)
            for j in range(4):
                rows = slice(512 * j, 512 * j + 512)
                pair = jnp.concatenate([st[l, c, rows, :], st[l, c + 1, rows, :]], axis=1)
                held[:, rows] += dot_t(lhs, pair)
            return 0

        lax.fori_loop(0, CAP // 2, contract, 0)
        delta = softplus(dt_pre + bias[l : l + 1, :])
        decay = jnp.exp(-delta * rate[l : l + 1, :])
        x_now = conv(l, x_pre, old and old[1], tail_x, conv_in)
        k_now = delta * jnp.sum(b_now * c_now, axis=1, keepdims=True) + skip[l : l + 1, :]
        if t == 0:
            kept[l] = (bc_pre, x_pre, b_now, x_now, delta, decay)
            k_state = decay
        else:
            _, _, b_old, x_old, delta_old, decay_old = old
            k_state = decay * decay_old
            k_old = decay * delta_old * jnp.sum(b_old * c_now, axis=1, keepdims=True)
        outs = []
        for h in range(16):
            cols = slice(128 * h, 128 * h + 128)
            one = slice(h, h + 1)
            y = k_state[:, one] * held[:, cols] + k_now[:, one] * x_now[:, cols]
            if t == 1:
                y += k_old[:, one] * x_old[:, cols]
            outs.append(y)
        gated = jnp.concatenate(outs, axis=1) * silu(gm * scale)
        mean_sq = jnp.sum(gated * gated, axis=1, keepdims=True) * (1.0 / CH)
        normed = (gated * lax.rsqrt(mean_sq + EPS) * out_gain[l : l + 1, :]).astype(BF16)
        for half in (0, 1):
            quarters = [normed[:, 1024 * half + 256 * i : 1024 * half + 256 * i + 256] for i in range(4)]
            gat[l, t, half, mine[1 - half], mine[half]] = dot(compact, jnp.concatenate(quarters, axis=0)).astype(BF16)
            gather(l, t, 0, half)

    def gather(l, t, stage, half):
        a, b = mine[1 - half], mine[half]
        axis = half if stage == 0 else 1 - half
        sems = (gsend_sem.at[t, stage, half], grecv_sem.at[t, stage, half])
        here = gat.at[l, t, half, a, b] if stage == 0 else gat.at[l, t, half, a]
        for k in (2, 1, 3):
            copy(here, here, *sems, (peer(axis, k), head)).start()
        three = gat.at[l, t, half, a, 0:3] if stage == 0 else gat.at[l, t, half, 0:3]
        flights[l, t, 3 + stage, half] = copy(three, three, *sems, (peer(axis, 1), head))

    def forward(l, t):
        for half in (0, 1):
            flights[l, t, 3, half].wait_recv()
            gather(l, t, 1, half)

    def to_heads(l, t, stage):
        sems = (hsend_sem.at[t, stage], hrecv_sem.at[t, stage])
        for k in (4, 3, 5, 2, 6, 1, 7):
            to = (head + k) % 8
            pair = (hs.at[l, t, to], hr.at[l, t, head]) if stage == 0 else (fin.at[l, t, head], fin.at[l, t, head])
            copy(*pair, *sems, (req, to)).start()
        seven = (hs.at[l, t, 0:7], hr.at[l, t, 0:7]) if stage == 0 else (fin.at[l, t, 0:7], fin.at[l, t, 0:7])
        flights[l, t, 5 + stage, 0] = copy(*seven, *sems, (req, (head + 1) % 8))

    def output(l, t):
        ready(l, 5)
        part = None
        for half in (0, 1):
            flights[l, t, 4, half].wait_recv()
            rows = gat[l, t, half].reshape(768, 256)
            lhs = jnp.concatenate([dot(back[half, sub], rows).astype(BF16) for sub in range(4)], axis=1)
            more = dot(lhs, wo[l, 1024 * half : 1024 * half + 1024, :])
            part = more if part is None else part + more
        for h in range(8):
            i, c = h // 4, h % 4
            hs[l, t, h] = part[48 * i : 48 * i + 48, 128 * c : 128 * c + 128].astype(BF16)
        to_heads(l, t, 0)

    def reduce(l, t):
        total = hs[l, t, head].astype(F32)
        flights[l, t, 5, 0].wait_recv()
        for k in range(1, 8):
            total += hr[l, t, (head + k) % 8].astype(F32)
        fin[l, t, head] = total.astype(BF16)
        to_heads(l, t, 1)

    def finish(l, t):
        flights[l, t, 6, 0].wait_recv()
        for h in range(8):
            i, c = h // 4, h % 4
            rows, cols = slice(48 * i, 48 * i + 48), slice(128 * c, 128 * c + 128)
            now = stream[t, rows, cols] + fin[l, t, h].astype(F32)
            if l < L - 1:
                stream[t, rows, cols] = now
            else:
                out[t, rows, cols] = now.astype(BF16)

    project(0, (0, 1))
    tables()
    for c in later:
        c.wait()
    t = iota((96, 1), 0)
    tl = div48(t)
    tk = (t - 48 * tl) >> 4
    by_layer = hot((iota((96, 72), 1) == (t & 15) * 6 + 2 * tk + tl) & ((t & 15) < CAP))
    for tails, rows in ((tail_x2, tail_x), (tail_bc2, tail_bc)):
        for i in range(36):
            rows[2 * i : 2 * i + 2, :] = tails[i].astype(F32)
        rows[...] = dot(by_layer, rows[0:72, :].astype(BF16))
    for l in range(L):
        second(l, 0)
        second(l, 1)
        if l == 0:
            for c in loads[1]:
                c.start()
        third(l, 0)
        drain(l, 0, 0)
        third(l, 1)
        drain(l, 1, 0)
        scan(l, 0)
        scan(l, 1)
        forward(l, 0)
        drain(l, 0, 1)
        drain(l, 0, 2)
        drain(l, 1, 1)
        drain(l, 1, 2)
        forward(l, 1)
        drain(l, 0, 3)
        drain(l, 1, 3)
        output(l, 0)
        output(l, 1)
        drain(l, 0, 4)
        reduce(l, 0)
        drain(l, 1, 4)
        reduce(l, 1)
        drain(l, 0, 5)
        finish(l, 0)
        if l < L - 1:
            project(l + 1, (0,))
        drain(l, 1, 5)
        finish(l, 1)
        if l < L - 1:
            project(l + 1, (1,))
        drain(l, 0, 6)
        drain(l, 1, 6)
    for key in list(flights):
        drain(*key[:3])


def on_device(
    embedded,
    ssm_states,
    conv_tail_x,
    conv_tail_bc,
    prefill_slot,
    decode_slot,
    norm_gain,
    w_gate,
    w_input,
    w_groups,
    w_step,
    conv_input,
    conv_groups,
    step_bias,
    decay_rate,
    skip_gain,
    out_gain,
    w_output,
):
    vmem = pl.BlockSpec(memory_space=pltpu.VMEM)
    hbm = pl.BlockSpec(memory_space=pl.ANY)

    def by_slot(tails):
        return jnp.transpose(tails, (1, 2, 0, 3)).reshape(CAP * 3, L, tails.shape[3])

    return pl.pallas_call(
        body,
        out_shape=jax.ShapeDtypeStruct((2, 96, WIDTH), BF16),
        in_specs=[hbm] * 18,
        out_specs=vmem,
        scratch_shapes=[
            pltpu.VMEM((2, 96, WIDTH), BF16),
            pltpu.VMEM((3 * CAP, L, CH), BF16),
            pltpu.VMEM((3 * CAP, L, 256), BF16),
            pltpu.VMEM((1, 96), jnp.int32),
            pltpu.VMEM((1, 96), jnp.int32),
            pltpu.VMEM((L, WIDTH), F32),
            pltpu.VMEM((L, 4, CH), F32),
            pltpu.VMEM((L, 4, 256), F32),
            pltpu.VMEM((L, 16), F32),
            pltpu.VMEM((L, 16), F32),
            pltpu.VMEM((L, 16), F32),
            pltpu.VMEM((L, CH), F32),
            pltpu.VMEM((96, CH), F32),
            pltpu.VMEM((96, 256), F32),
            pltpu.SemaphoreType.DMA((12,)),
            pltpu.VMEM((L, WIDTH, CH), BF16),
            pltpu.VMEM((L, WIDTH, CH), BF16),
            pltpu.VMEM((L, WIDTH, 256), BF16),
            pltpu.VMEM((L, 16, WIDTH), BF16),
            pltpu.VMEM((L, CH, WIDTH), BF16),
            pltpu.VMEM((L, CAP, CH, 128), BF16),
            pltpu.VMEM((S, ROWS, WIDTH), F32),
            pltpu.VMEM((ROWS, ROWS), BF16),
            pltpu.VMEM((128, 48), BF16),
            pltpu.VMEM((128, 48), BF16),
            pltpu.VMEM((32, 32), BF16),
            pltpu.VMEM((32, 32), BF16),
            pltpu.VMEM((2, 4, ROWS, 768), BF16),
            pltpu.VMEM((L, S, 2, 4, 48, PART), BF16),
            pltpu.VMEM((L, S, 2, 4, 48, PART), BF16),
            pltpu.VMEM((L, S, 2, 4, 32, PART), BF16),
            pltpu.VMEM((L, S, 2, 4, 32, PART), BF16),
            pltpu.VMEM((L, S, 2, 4, 8, PART), F32),
            pltpu.VMEM((L, S, 2, 4, 8, PART), F32),
            pltpu.VMEM((L, S, 2, 4, 4, 48, 256), BF16),
            pltpu.VMEM((16, CH), F32),
            pltpu.VMEM((L, S, 8, 48, 128), BF16),
            pltpu.VMEM((L, S, 8, 48, 128), BF16),
            pltpu.VMEM((L, S, 8, 48, 128), BF16),
            pltpu.SemaphoreType.DMA((L, 6)),
            pltpu.SemaphoreType.DMA((S, 6)),
            pltpu.SemaphoreType.DMA((S, 6)),
            pltpu.SemaphoreType.DMA((S, 2, 2)),
            pltpu.SemaphoreType.DMA((S, 2, 2)),
            pltpu.SemaphoreType.DMA((S, 2)),
            pltpu.SemaphoreType.DMA((S, 2)),
        ],
        compiler_params=pltpu.CompilerParams(
            collective_id=0, has_side_effects=True, vmem_limit_bytes=58 * 2**20
        ),
    )(
        embedded,
        ssm_states.reshape(L, CAP, CH, 128),
        by_slot(conv_tail_x),
        by_slot(conv_tail_bc),
        prefill_slot.reshape(1, 96),
        decode_slot.reshape(1, 96),
        norm_gain,
        w_gate,
        w_input,
        w_groups,
        jnp.swapaxes(w_step, 1, 2),
        conv_input,
        conv_groups,
        step_bias,
        decay_rate,
        skip_gain,
        out_gain,
        w_output,
    )


def solution(mesh):
    return jax.shard_map(
        on_device,
        mesh=mesh,
        in_specs=(
            P(None, None, "req"),
            P(None, "req", "head", None, None),
            P(None, "req", None, "head"),
            P(None, "req", None, "head"),
            P(),
            P(),
            P(None, "req"),
            P(None, "req", "head"),
            P(None, "req", "head"),
            P(None, "req", "head"),
            P(None, "req", "head"),
            P(None, None, "head"),
            P(None, None, "head"),
            P(None, "head"),
            P(None, "head"),
            P(None, "head"),
            P(None, "head"),
            P(None, "head", "req"),
        ),
        out_specs=P(None, None, "req"),
        check_vma=False,
    )
```

```python
import jax
import jax.numpy as jnp
from jax import lax
from jax.experimental import pallas as pl
from jax.experimental.pallas import tpu as pltpu
from jax.sharding import PartitionSpec as P

MESH = pl.DeviceIdType.MESH
F32 = jnp.float32
BF16 = jnp.bfloat16
EPS = 1e-05

L = 2
D = 8192
ROWS = 96
WIDTH = 512
CH = 2048
S = 2
PART = 1024
EXT = 256
CAP = 12


def iota(shape, dim):
    return lax.broadcasted_iota(jnp.int32, shape, dim)


def div6(v):
    return (v * 43691) >> 18


def div12(v):
    return (v * 43691) >> 19


def div24(v):
    return (v * 43691) >> 20


def div48(v):
    return (v * 43691) >> 21


def hot(cond):
    return jnp.where(cond, 1.0, 0.0).astype(BF16)


def dot(a, b):
    return jnp.dot(a, b, preferred_element_type=F32)


def dot_t(a, b):
    return lax.dot_general(a, b, (((1,), (1,)), ((), ())), preferred_element_type=F32)


def silu(v):
    return v / (1.0 + jnp.exp(-v))


def softplus(v):
    return jnp.maximum(v, 0.0) + jnp.log(1.0 + jnp.exp(-jnp.abs(v)))


def body(
    emb_h,
    states,
    tail_x_h,
    tail_bc_h,
    pslot_h,
    dslot_h,
    norm_gain_h,
    w_gate,
    w_input,
    w_groups,
    w_step,
    conv_in_h,
    conv_grp_h,
    bias_h,
    rate_h,
    skip_h,
    out_gain_h,
    w_output,
    out,
    emb,
    tail_x2,
    tail_bc2,
    pslot,
    dslot,
    norm_gain,
    conv_in,
    conv_grp,
    bias,
    rate,
    skip,
    out_gain,
    tail_x,
    tail_bc,
    small_sem,
    wg,
    wi,
    wb,
    ws,
    wo,
    st,
    stream,
    perm_b,
    sel_a,
    sel_b,
    pick_a,
    pick_b,
    back,
    e1s,
    e1r,
    e2s,
    e2r,
    e3s,
    e3r,
    s1s,
    s1r,
    s2s,
    s2r,
    s3s,
    s3r,
    gat,
    held,
    hx,
    hr,
    hy,
    fin,
    load_sem,
    send_sem,
    recv_sem,
    gsend_sem,
    grecv_sem,
    hsend_sem,
    hrecv_sem,
):
    req = lax.axis_index("req")
    head = lax.axis_index("head")
    z = req // 4
    x = req % 4
    mine = (z, x)
    y = head // 2
    core = head % 2
    partner = head + 1 - 2 * core

    def peer(axis, k):
        if axis == 0:
            return ((z + k) % 4) * 4 + x
        return z * 4 + (x + k) % 4

    loads = []
    for l in range(L):
        row = [
            (w_step.at[l], ws.at[l]),
            (w_groups.at[l], wb.at[l]),
            (w_gate.at[l], wg.at[l]),
            (w_input.at[l], wi.at[l]),
            (states.at[l], st.at[l]),
            (w_output.at[l], wo.at[l]),
        ]
        loads.append([pltpu.make_async_copy(a, b, load_sem.at[l, i]) for i, (a, b) in enumerate(row)])
    first = [(pslot_h, pslot), (dslot_h, dslot), (emb_h, emb), (norm_gain_h, norm_gain)]
    later = [
        (tail_x_h, tail_x2),
        (tail_bc_h, tail_bc2),
        (conv_in_h, conv_in),
        (conv_grp_h, conv_grp),
        (bias_h, bias),
        (rate_h, rate),
        (skip_h, skip),
        (out_gain_h, out_gain),
    ]
    first = [pltpu.make_async_copy(a, b, small_sem.at[i]) for i, (a, b) in enumerate(first)]
    later = [pltpu.make_async_copy(a, b, small_sem.at[4 + i]) for i, (a, b) in enumerate(later)]
    for c in first + loads[0] + later:
        c.start()

    barrier = pltpu.get_barrier_semaphore()
    for k in (1, 2, 3):
        for axis in (0, 1):
            pl.semaphore_signal(barrier, inc=1, device_id=(peer(axis, k), head), device_id_type=MESH)
    for to in (partner, (head + 2) % 8, (head + 4) % 8, (head + 6) % 8):
        pl.semaphore_signal(barrier, inc=1, device_id=(req, to), device_id_type=MESH)

    for c in first:
        c.wait()

    for t in range(S):
        stream[t] = emb[t].astype(F32)

    prow = pslot[...]
    drow = dslot[...]
    diag = iota((96, 96), 0) == iota((96, 96), 1)
    pcol = jnp.sum(jnp.where(diag, prow, 0), axis=1, keepdims=True)
    dcol = jnp.sum(jnp.where(diag, drow, 0), axis=1, keepdims=True)

    n = iota((1, ROWS), 1)
    g = div24(n)
    j = n - 24 * g
    jx = div6(j)
    perm_b[...] = hot(iota((ROWS, ROWS), 0) == 24 * jx + 6 * g + (j - 6 * jx))

    k = iota((1, 48), 1)
    kp = div24(k)
    kj = k - 24 * kp
    kg = div6(kj)
    p = iota((128, 1), 0)
    for half in (0, 1):
        r = 24 * z + kj if half == 0 else 24 * kg + 6 * x + (kj - 6 * kg)
        slot = jnp.sum(jnp.where(dcol == r, pcol, 0), axis=0, keepdims=True)
        q = div12(slot)
        first, second = p >> 5, (p >> 3) & 3
        pq = 4 * second + first if half == 0 else 4 * first + second
        key = (pq * 4 + (p & 3)) * 2 + ((p >> 2) & 1)
        (sel_a if half == 0 else sel_b)[...] = hot(key == (q * 4 + kg) * 2 + kp)

    def tables():
        t = iota((32, 1), 0)
        c = t & 15
        owner = jnp.sum(jnp.where(prow == CAP * req + c, div6(drow) + 1, 0), axis=1, keepdims=True) - 1
        mine_key = jnp.where((owner >= 0) & (c < CAP), owner * 2 + (t >> 4), -1)
        u = iota((1, 32), 1)
        src, up, other = u >> 3, (u >> 2) & 1, u & 3
        for half in (0, 1):
            key = (4 * src + other if half == 0 else 4 * other + src) * 2 + up
            (pick_a if half == 0 else pick_b)[...] = hot(mine_key == key)
        want = jnp.sum(jnp.where(drow == iota((ROWS, 1), 0), prow, 0), axis=1, keepdims=True)
        v = iota((1, 768), 1)
        blk = div48(v)
        vw = v - 48 * blk
        vsub = div12(vw)
        vc = vw - 12 * vsub
        for half in (0, 1):
            q = (blk & 3) * 4 + (blk >> 2) if half == 0 else blk
            for sub in range(4):
                back[half, sub] = hot(want == jnp.where(vsub == sub, CAP * q + vc, -1))

    wr = iota((48, 1), 0)
    wsub = div12(wr)
    compact = hot(iota((48, 64), 1) == 16 * wsub + (wr - 12 * wsub))

    place = hot(iota((16, 128), 0) == iota((16, 128), 1))

    pl.semaphore_wait(barrier, 10)

    def drain(l, t, phase):
        for part in (0, 1, 2):
            f = flights.pop((l, t, phase, part), None)
            if f is not None:
                f.wait_send()

    def copy(src, dst, ss, rs, dev):
        return pltpu.make_async_remote_copy(
            src_ref=src, dst_ref=dst, send_sem=ss, recv_sem=rs, device_id=dev, device_id_type=MESH
        )

    flights = {}

    def exchange(l, t, phase, part):
        pairs = ((s1s, s1r), (s2s, s2r), (s3s, s3r)) if part < 2 else ((e1s, e1r), (e2s, e2r), (e3s, e3r))
        send, recv = (ref.at[l, t, part] if part < 2 else ref.at[l, t] for ref in pairs[phase])
        axis = (phase + part) % 2
        me = mine[axis]
        e = 3 * phase + part
        sems = (send_sem.at[t, e], recv_sem.at[t, e])
        for k in (2, 1, 3):
            copy(send.at[(me + k) % 4], recv.at[me], *sems, (peer(axis, k), head)).start()
        flights[l, t, phase, part] = copy(send.at[0:3], recv.at[0:3], *sems, (peer(axis, 1), head))

    def summed(l, t, phase, part):
        pairs = ((s1s, s1r), (s2s, s2r)) if part < 2 else ((e1s, e1r), (e2s, e2r))
        send, recv = (ref.at[l, t, part] if part < 2 else ref.at[l, t] for ref in pairs[phase])
        me = mine[(phase + part) % 2]
        flights[l, t, phase, part].wait_recv()
        total = send[me].astype(F32)
        for k in (1, 2, 3):
            total += recv[(me + k) % 4].astype(F32)
        return total

    waited = set()

    def ready(l, i):
        if (l, i) not in waited:
            waited.add((l, i))
            loads[l][i].wait()

    def project(l, steps):
        many = len(steps)
        x_now = jnp.concatenate([stream[t] for t in steps], axis=0)
        lhs_a = (x_now * norm_gain[l : l + 1, :]).astype(BF16)
        squares = jnp.sum(x_now * x_now, axis=1, keepdims=True)

        def put(half, cols, low, high):
            for i, t in enumerate(steps):
                for g in range(4):
                    rows = slice(ROWS * i + 24 * g, ROWS * i + 24 * g + 24)
                    s1s[l, t, half, g, :, cols] = jnp.concatenate([low[rows], high[rows]], axis=0).astype(BF16)

        def main(half, lhs, weight):
            def tile(i, _):
                at = pl.multiple_of(i * 256, 256)
                low = dot(lhs, weight[l, :, pl.ds(at, 256)])
                high = dot(lhs, weight[l, :, pl.ds(pl.multiple_of(at + 1024, 256), 256)])
                put(half, pl.ds(at, 256), low, high)
                return 0

            lax.fori_loop(0, 4, tile, 0)

        ready(l, 0)
        small = dot(dot_t(lhs_a, ws[l]).astype(BF16), place)
        small = jnp.where(iota((ROWS * many, 128), 1) == 16, squares, small)
        ready(l, 1)
        bc = dot(lhs_a, wb[l])
        low = jnp.concatenate([small, bc[:, :128]], axis=1)
        high = jnp.concatenate([jnp.zeros_like(small), bc[:, 128:]], axis=1)
        for i, t in enumerate(steps):
            for g in range(4):
                rows = slice(ROWS * i + 24 * g, ROWS * i + 24 * g + 24)
                e1s[l, t, g] = jnp.concatenate([low[rows], high[rows]], axis=0).astype(BF16)
            exchange(l, t, 0, 2)
        ready(l, 2)
        main(0, lhs_a, wg)
        if many == 1:
            exchange(l, steps[0], 0, 0)
        ready(l, 3)
        lhs_b = jnp.concatenate(
            [dot(perm_b[...], lhs_a[ROWS * i : ROWS * i + ROWS]).astype(BF16) for i in range(many)], axis=0
        )
        main(1, lhs_b, wi)
        for t in steps:
            if many > 1:
                exchange(l, t, 0, 0)
            exchange(l, t, 0, 1)

    def second(l, t, parts):
        for part in parts:
            sel = (sel_b if part == 1 else sel_a)[...]
            put = dot(sel, summed(l, t, 0, part).astype(BF16)).astype(BF16)
            for g in range(4):
                if part < 2:
                    s2s[l, t, part, g] = put[32 * g : 32 * g + 32]
                else:
                    e2s[l, t, g] = put[32 * g : 32 * g + 32]
            exchange(l, t, 1, part)

    def third(l, t, parts):
        for part in parts:
            total = summed(l, t, 1, part)
            for g in range(4):
                if part < 2:
                    s3s[l, t, part, g] = total[8 * g : 8 * g + 8]
                else:
                    e3s[l, t, g] = total[8 * g : 8 * g + 8]
            exchange(l, t, 2, part)

    def landed(l, t, part):
        send, recv = (ref.at[l, t, part] if part < 2 else ref.at[l, t] for ref in ((s3s, s3r) if part < 2 else (e3s, e3r)))
        me = mine[part % 2]
        flights[l, t, 2, part].wait_recv()
        recv[me] = send[me]
        block = recv[...].reshape(32, recv.shape[2])
        pick = (pick_b if part == 1 else pick_a)[...]
        top = block.astype(BF16)
        rest = (block - top.astype(F32)).astype(BF16)
        both = dot(pick, top) + dot(pick, rest)
        return both[:16], both[16:]

    kept = {}

    def conv(l, pre, old, tails, taps):
        tap = [taps[l, i : i + 1, :] for i in range(4)]
        tail = [tails[48 * l + 16 * i : 48 * l + 16 * i + 16, :] for i in range(3)]
        seq = (tail + [pre]) if old is None else (tail[1:] + [old.astype(BF16).astype(F32), pre])
        return silu(seq[0] * tap[0] + seq[1] * tap[1] + seq[2] * tap[2] + seq[3] * tap[3])

    def early(l, t):
        low, high = landed(l, t, 2)
        small = low[:, :128]
        scale = lax.rsqrt(small[:, 16:17] * (1.0 / D) + EPS)
        delta = softplus(small[:, :16] * scale + bias[l : l + 1, :])
        decay = jnp.exp(-delta * rate[l : l + 1, :])
        bc_pre = jnp.concatenate([low[:, 128:], high[:, 128:]], axis=1) * scale
        bc = conv(l, bc_pre, kept[l, 0][4] if t else None, tail_bc, conv_grp)
        b_now, c_now = bc[:, :128], bc[:, 128:]
        k_now = delta * jnp.sum(b_now * c_now, axis=1, keepdims=True) + skip[l : l + 1, :]
        if t == 0:
            k_state, k_old = decay, None
        else:
            _, delta_old, decay_old, b_old = kept[l, 0][:4]
            k_state = decay * decay_old
            k_old = decay * delta_old * jnp.sum(b_old * c_now, axis=1, keepdims=True)
        kept[l, t] = (scale, delta, decay, b_now, bc_pre, k_state, k_now, k_old)
        kept[l, t, "c"] = c_now.astype(BF16)

    def contract(l):
        both_c = jnp.concatenate([kept[l, 0, "c"], kept[l, 1, "c"]], axis=0)
        slot_of = iota((32, 1), 0) & 15
        zero = jnp.zeros((), BF16)
        ready(l, 4)
        held[...] = jnp.zeros((32, CH), F32)

        def pair_of(i, _):
            c = 2 * i
            lhs = jnp.concatenate([jnp.where(slot_of == c, both_c, zero), jnp.where(slot_of == c + 1, both_c, zero)], axis=1)
            for j in range(4):
                rows = slice(512 * j, 512 * j + 512)
                pair = jnp.concatenate([st[l, c, rows, :], st[l, c + 1, rows, :]], axis=1)
                held[:, rows] += dot_t(lhs, pair)
            return 0

        lax.fori_loop(0, CAP // 2, pair_of, 0)

    def scan(l, t):
        scale, k_state, k_now, k_old = (kept[l, t][i] for i in (0, 5, 6, 7))
        x_pre = jnp.concatenate(landed(l, t, 1), axis=1) * scale
        x_old_pre, x_old = kept.get((l, "x"), (None, None))
        x_now = conv(l, x_pre, x_old_pre, tail_x, conv_in)
        kept[l, "x"] = (x_pre, x_now)
        outs = []
        for h in range(16):
            cols = slice(128 * h, 128 * h + 128)
            one = slice(h, h + 1)
            y = k_state[:, one] * held[16 * t : 16 * t + 16, cols] + k_now[:, one] * x_now[:, cols]
            if t == 1:
                y += k_old[:, one] * x_old[:, cols]
            outs.append(y)
        gate_pre = jnp.concatenate(landed(l, t, 0), axis=1) * scale
        gated = jnp.concatenate(outs, axis=1) * silu(gate_pre)
        mean_sq = jnp.sum(gated * gated, axis=1, keepdims=True) * (1.0 / CH)
        normed = (gated * lax.rsqrt(mean_sq + EPS) * out_gain[l : l + 1, :]).astype(BF16)
        for half in (0, 1):
            quarters = [normed[:, 1024 * half + 256 * i : 1024 * half + 256 * i + 256] for i in range(4)]
            gat[l, t, half, mine[1 - half], mine[half]] = dot(compact, jnp.concatenate(quarters, axis=0)).astype(BF16)
            gather(l, t, 0, half)

    def gather(l, t, stage, half):
        a, b = mine[1 - half], mine[half]
        axis = half if stage == 0 else 1 - half
        sems = (gsend_sem.at[t, stage, half], grecv_sem.at[t, stage, half])
        here = gat.at[l, t, half, a, b] if stage == 0 else gat.at[l, t, half, a]
        for k in (2, 1, 3):
            copy(here, here, *sems, (peer(axis, k), head)).start()
        three = gat.at[l, t, half, a, 0:3] if stage == 0 else gat.at[l, t, half, 0:3]
        flights[l, t, 3 + stage, half] = copy(three, three, *sems, (peer(axis, 1), head))

    def forward(l, t):
        for half in (0, 1):
            flights[l, t, 3, half].wait_recv()
            gather(l, t, 1, half)

    def output(l, t):
        ready(l, 5)
        part = None
        for half in (0, 1):
            flights[l, t, 4, half].wait_recv()
            rows = gat[l, t, half].reshape(768, 256)
            lhs = jnp.concatenate([dot(back[half, sub], rows).astype(BF16) for sub in range(4)], axis=1)
            more = dot(lhs, wo[l, 1024 * half : 1024 * half + 1024, :])
            part = more if part is None else part + more
        low, high = part[:48], part[48:]
        hx[l, t, 0] = jnp.where(core == 0, low, high)
        hx[l, t, 1] = jnp.where(core == 0, high, low)
        f = copy(hx.at[l, t, 1], hr.at[l, t], hsend_sem.at[l, t, 0], hrecv_sem.at[l, t, 0], (req, partner))
        f.start()
        flights[l, t, 5, 0] = f

    def reduce(l, t):
        flights[l, t, 5, 0].wait_recv()
        hy[l, t, y] = (hx[l, t, 0] + hr[l, t]).astype(BF16)
        sems = (hsend_sem.at[l, t, 1], hrecv_sem.at[l, t, 1])
        for k in (2, 1, 3):
            copy(hy.at[l, t, y], hy.at[l, t, y], *sems, (req, (head + 2 * k) % 8)).start()
        three = hy.at[l, t, 0:3]
        flights[l, t, 6, 0] = copy(three, three, *sems, (req, (head + 2) % 8))

    def finish(l, t):
        flights[l, t, 6, 0].wait_recv()
        total = hy[l, t, 0].astype(F32)
        for i in (1, 2, 3):
            total += hy[l, t, i].astype(F32)
        fin[l, t, core] = total
        f = copy(fin.at[l, t, core], fin.at[l, t, core], hsend_sem.at[l, t, 2], hrecv_sem.at[l, t, 2], (req, partner))
        f.start()
        flights[l, t, 7, 0] = f

    def close(l, t):
        flights[l, t, 7, 0].wait_recv()
        if l < L - 1:
            stream[t] += fin[l, t].reshape(ROWS, WIDTH)
        else:
            out[t] = (stream[t] + fin[l, t].reshape(ROWS, WIDTH)).astype(BF16)

    project(0, (0, 1))
    tables()
    for c in later:
        c.wait()
    t = iota((96, 1), 0)
    tl = div48(t)
    tk = (t - 48 * tl) >> 4
    by_layer = hot((iota((96, 72), 1) == (t & 15) * 6 + 2 * tk + tl) & ((t & 15) < CAP))
    for tails, rows in ((tail_x2, tail_x), (tail_bc2, tail_bc)):
        for i in range(36):
            rows[2 * i : 2 * i + 2, :] = tails[i].astype(F32)
        rows[...] = dot(by_layer, rows[0:72, :].astype(BF16))
    second(0, 0, (2,))
    second(0, 1, (2,))
    for l in range(L):
        last = l == L - 1
        second(l, 0, (0, 1))
        if l:
            second(l, 1, (2,))
        third(l, 0, (2,))
        second(l, 1, (0, 1))
        if l == 0:
            for c in loads[1]:
                c.start()
        third(l, 1, (2,))
        drain(l, 0, 0)
        drain(l, 1, 0)
        third(l, 0, (0, 1))
        early(l, 0)
        early(l, 1)
        third(l, 1, (0, 1))
        contract(l)
        scan(l, 0)
        scan(l, 1)
        forward(l, 0)
        for phase in (1, 2):
            drain(l, 0, phase)
            drain(l, 1, phase)
        forward(l, 1)
        drain(l, 0, 3)
        drain(l, 1, 3)
        output(l, 0)
        reduce(l, 0)
        output(l, 1)
        drain(l, 0, 4)
        drain(l, 0, 5)
        if last:
            reduce(l, 1)
            finish(l, 0)
        else:
            finish(l, 0)
            reduce(l, 1)
        close(l, 0)
        if not last:
            project(l + 1, (0,))
        drain(l, 1, 4)
        drain(l, 1, 5)
        drain(l, 0, 6)
        drain(l, 0, 7)
        finish(l, 1)
        close(l, 1)
        if not last:
            second(l + 1, 0, (2,))
            project(l + 1, (1,))
        drain(l, 1, 6)
        drain(l, 1, 7)
    for key in list(flights):
        drain(*key[:3])


def on_device(
    embedded,
    ssm_states,
    conv_tail_x,
    conv_tail_bc,
    prefill_slot,
    decode_slot,
    norm_gain,
    w_gate,
    w_input,
    w_groups,
    w_step,
    conv_input,
    conv_groups,
    step_bias,
    decay_rate,
    skip_gain,
    out_gain,
    w_output,
):
    vmem = pl.BlockSpec(memory_space=pltpu.VMEM)
    hbm = pl.BlockSpec(memory_space=pl.ANY)

    def by_slot(tails):
        return jnp.transpose(tails, (1, 2, 0, 3)).reshape(CAP * 3, L, tails.shape[3])

    return pl.pallas_call(
        body,
        out_shape=jax.ShapeDtypeStruct((2, 96, WIDTH), BF16),
        in_specs=[hbm] * 18,
        out_specs=vmem,
        scratch_shapes=[
            pltpu.VMEM((2, 96, WIDTH), BF16),
            pltpu.VMEM((3 * CAP, L, CH), BF16),
            pltpu.VMEM((3 * CAP, L, 256), BF16),
            pltpu.VMEM((1, 96), jnp.int32),
            pltpu.VMEM((1, 96), jnp.int32),
            pltpu.VMEM((L, WIDTH), F32),
            pltpu.VMEM((L, 4, CH), F32),
            pltpu.VMEM((L, 4, 256), F32),
            pltpu.VMEM((L, 16), F32),
            pltpu.VMEM((L, 16), F32),
            pltpu.VMEM((L, 16), F32),
            pltpu.VMEM((L, CH), F32),
            pltpu.VMEM((96, CH), F32),
            pltpu.VMEM((96, 256), F32),
            pltpu.SemaphoreType.DMA((12,)),
            pltpu.VMEM((L, WIDTH, CH), BF16),
            pltpu.VMEM((L, WIDTH, CH), BF16),
            pltpu.VMEM((L, WIDTH, 256), BF16),
            pltpu.VMEM((L, 16, WIDTH), BF16),
            pltpu.VMEM((L, CH, WIDTH), BF16),
            pltpu.VMEM((L, CAP, CH, 128), BF16),
            pltpu.VMEM((S, ROWS, WIDTH), F32),
            pltpu.VMEM((ROWS, ROWS), BF16),
            pltpu.VMEM((128, 48), BF16),
            pltpu.VMEM((128, 48), BF16),
            pltpu.VMEM((32, 32), BF16),
            pltpu.VMEM((32, 32), BF16),
            pltpu.VMEM((2, 4, ROWS, 768), BF16),
            pltpu.VMEM((L, S, 4, 48, EXT), BF16),
            pltpu.VMEM((L, S, 4, 48, EXT), BF16),
            pltpu.VMEM((L, S, 4, 32, EXT), BF16),
            pltpu.VMEM((L, S, 4, 32, EXT), BF16),
            pltpu.VMEM((L, S, 4, 8, EXT), F32),
            pltpu.VMEM((L, S, 4, 8, EXT), F32),
            pltpu.VMEM((L, S, 2, 4, 48, PART), BF16),
            pltpu.VMEM((L, S, 2, 4, 48, PART), BF16),
            pltpu.VMEM((L, S, 2, 4, 32, PART), BF16),
            pltpu.VMEM((L, S, 2, 4, 32, PART), BF16),
            pltpu.VMEM((L, S, 2, 4, 8, PART), F32),
            pltpu.VMEM((L, S, 2, 4, 8, PART), F32),
            pltpu.VMEM((L, S, 2, 4, 4, 48, 256), BF16),
            pltpu.VMEM((32, CH), F32),
            pltpu.VMEM((L, S, 2, 48, WIDTH), F32),
            pltpu.VMEM((L, S, 48, WIDTH), F32),
            pltpu.VMEM((L, S, 4, 48, WIDTH), BF16),
            pltpu.VMEM((L, S, 2, 48, WIDTH), F32),
            pltpu.SemaphoreType.DMA((L, 6)),
            pltpu.SemaphoreType.DMA((S, 9)),
            pltpu.SemaphoreType.DMA((S, 9)),
            pltpu.SemaphoreType.DMA((S, 2, 2)),
            pltpu.SemaphoreType.DMA((S, 2, 2)),
            pltpu.SemaphoreType.DMA((L, S, 3)),
            pltpu.SemaphoreType.DMA((L, S, 3)),
        ],
        compiler_params=pltpu.CompilerParams(
            collective_id=0, has_side_effects=True, vmem_limit_bytes=58 * 2**20
        ),
    )(
        embedded,
        ssm_states.reshape(L, CAP, CH, 128),
        by_slot(conv_tail_x),
        by_slot(conv_tail_bc),
        prefill_slot.reshape(1, 96),
        decode_slot.reshape(1, 96),
        norm_gain,
        w_gate,
        w_input,
        w_groups,
        jnp.swapaxes(w_step, 1, 2),
        conv_input,
        conv_groups,
        step_bias,
        decay_rate,
        skip_gain,
        out_gain,
        w_output,
    )


def solution(mesh):
    return jax.shard_map(
        on_device,
        mesh=mesh,
        in_specs=(
            P(None, None, "req"),
            P(None, "req", "head", None, None),
            P(None, "req", None, "head"),
            P(None, "req", None, "head"),
            P(),
            P(),
            P(None, "req"),
            P(None, "req", "head"),
            P(None, "req", "head"),
            P(None, "req", "head"),
            P(None, "req", "head"),
            P(None, None, "head"),
            P(None, None, "head"),
            P(None, "head"),
            P(None, "head"),
            P(None, "head"),
            P(None, "head"),
            P(None, "head", "req"),
        ),
        out_specs=P(None, None, "req"),
        check_vma=False,
    )
```
